32 devices in a mesh: grp: 2 (over y), blk: 8 (over z, x), tch: 2 (over core).
Axes of the slice: x: 2, y: 2, z: 4, core: 2. Of those that a mesh axis runs over, the one named last changes fastest.
Arguments:
- samples: bfloat16 [4, 32, 65536], P('grp', 'blk', 'tch'), parts along dimension 0, may hold values from -6 to 6
- history: bfloat16 [4, 32, 15360], P('grp', 'blk'), parts along dimension 0, may hold values from -6 to 6
- coefficients: float32 [16, 1024], replicated, may hold values from -1.5 to 1.5
- station_of_slot: int32 [32], P('grp'), parts along dimension 0, may hold values from 0 to 15, each once
- station_ok: int32 [32], P('grp'), parts along dimension 0, may hold values from 0 to 1, as said below
Outputs:
- visibilities: bfloat16 [4, 1024, 32, 32], P('grp', ('blk', 'tch')), parts along dimension 0
The draws below stay inside these ranges and needn't reach their ends.
There are 2 independent parts, one for each index of `grp`. The reference program is written for one: setup_inputs(seed, part) draws one part's arguments, and reference() takes and returns one part's arrays. A program takes and returns all parts, laid end to end along the dimension named above; an argument that names none is the same for every part. Nothing has to cross between parts.
Inputs may be any that keep to these rules, and one draw needn't show every extreme that they name: `station_of_slot`: each station stands in exactly one slot. `station_ok`: 2 or 3 stations are flagged.
All inputs are finite; a program needn't handle non-finite values.
Results may differ from the reference program's by a relative error of at most 0.0074.
Values may be sent and summed in bfloat16 or wider, within the bound.
A program may use at most 64 MiB of HBM per device.

```python
import math
import jax
import jax.numpy as jnp
from jax import lax

NFFT = 1024
TAPS = 16
STATIONS = 16
INPUTS = 32
NSPEC = 64


def draw_station_ok(key, part):
    flagged = STATIONS // 8 + part % 2
    order_vals = jax.random.permutation(jax.random.fold_in(key, 17), STATIONS).astype(jnp.int32)
    return (order_vals >= flagged).astype(jnp.int32)


def level_of(key, dims, split, low, high):
    gain = 1.0
    for dim, parts in split:
        steps = jax.random.uniform(jax.random.fold_in(jax.random.fold_in(key, 6), dim), (parts,), jnp.float32, low / len(split), high / len(split))
        gain = gain * jnp.repeat(jnp.exp(steps), dims[dim] // parts).reshape((-1,) + (1,) * (len(dims) - 1 - dim))
    return gain


def bell_draw(key, shape, width, bound, pieces=(), held_as=jnp.bfloat16):
    array = width * jax.random.normal(key, shape, jnp.float32)
    if pieces:
        array = array * level_of(key, shape, pieces, -0.22, 0.18)
    return jnp.clip(array, -bound, bound).astype(held_as)


def setup_inputs(seed: int = 0, part: int = 0) -> dict:
    key_of = jax.random.split(jax.random.key(seed), 6)
    part_splits = jax.random.split(jax.random.fold_in(key_of[5], part), 6)
    return {
        "samples": bell_draw(part_splits[0], (2, INPUTS, NSPEC * NFFT), 1.0, 6.0, ((1, 8), (2, 2))),
        "history": bell_draw(part_splits[1], (2, INPUTS, (TAPS - 1) * NFFT), 1.0, 6.0, ((1, 8),)),
        "coefficients": bell_draw(key_of[2], (TAPS, NFFT), TAPS ** -0.5, 1.5, (), jnp.float32),
        "station_of_slot": jax.random.permutation(part_splits[3], STATIONS).astype(jnp.int32),
        "station_ok": draw_station_ok(jax.random.fold_in(jax.random.fold_in(key_of[5], part), 71), part),
    }


def dft_table(fft_len):
    row_index = lax.broadcasted_iota(jnp.int32, (fft_len, fft_len), 0)
    col_index = lax.broadcasted_iota(jnp.int32, (fft_len, fft_len), 1)
    phase_step = row_index * col_index % fft_len
    angles = phase_step.astype(jnp.float32) * (2.0 * math.pi / fft_len)
    norm_scale = 1.0 / math.sqrt(fft_len)
    cosine = jnp.cos(angles) * norm_scale
    sine_part = jnp.sin(angles) * norm_scale
    upper_half = jnp.concatenate([cosine, -sine_part], axis=1)
    lower_half = jnp.concatenate([sine_part, cosine], axis=1)
    return jnp.concatenate([upper_half, lower_half], axis=0).astype(jnp.bfloat16)

def filter_bank(extended, coefficients, spec_count):
    tap_count, fft_len = coefficients.shape
    blocks = extended.reshape(extended.shape[0], extended.shape[1], -1, fft_len)
    running = jnp.zeros((extended.shape[0], extended.shape[1], spec_count, fft_len), jnp.float32)
    for tap_index in range(tap_count):
        running = running + coefficients[tap_index] * blocks[:, :, tap_index:tap_index + spec_count, :].astype(jnp.float32)
    return running.astype(jnp.bfloat16)

def channelize(filtered, dft_matrix):
    row_count, spec_count, fft_len = (filtered.shape[1], filtered.shape[2], filtered.shape[3])
    flat_rows = jnp.transpose(filtered, (1, 2, 0, 3)).reshape(row_count * spec_count, 2 * fft_len)
    product = jnp.dot(flat_rows, dft_matrix, preferred_element_type=jnp.float32).astype(jnp.bfloat16)
    return product.reshape(row_count, spec_count, 2, fft_len)

def reorder_inputs(values, station_of_slot, station_ok):
    station_count = station_of_slot.shape[0]
    input_count = values.shape[1]
    pol_count = input_count // station_count
    slot_index = jnp.zeros((station_count,), jnp.int32).at[station_of_slot].set(jnp.arange(station_count, dtype=jnp.int32))
    position = jnp.arange(input_count, dtype=jnp.int32)
    source_rows = (slot_index[position // pol_count] * pol_count + position % pol_count).astype(jnp.int32)
    keep_mask = station_ok[position // pol_count].astype(values.dtype)
    return jnp.take(values, source_rows, axis=1) * keep_mask[None, :, None]

def correlate(ordered, inverse_count):
    half_cols = ordered.shape[2] // 2
    rotated = jnp.concatenate([-ordered[:, :, half_cols:], ordered[:, :, :half_cols]], axis=2)
    real_vis = jnp.einsum('cak,cbk->cab', ordered, ordered)
    imag_vis = jnp.einsum('cak,cbk->cab', ordered, rotated)
    return (jnp.stack([real_vis, imag_vis], axis=0) * inverse_count).astype(jnp.bfloat16)

def reference(samples, history, coefficients, station_of_slot, station_ok):
    tap_count, fft_len = coefficients.shape
    spec_count = samples.shape[2] // fft_len
    extended = jnp.concatenate([history, samples], axis=2)
    filtered = filter_bank(extended, coefficients, spec_count)
    spectra = channelize(filtered, dft_table(fft_len))
    input_count = spectra.shape[0]
    channel_major = jnp.transpose(spectra, (3, 0, 2, 1)).reshape(fft_len, input_count, 2 * spec_count)
    ordered = reorder_inputs(channel_major, station_of_slot, station_ok)
    group_size = 8
    grouped = ordered.reshape(fft_len // group_size, group_size, input_count, 2 * spec_count)
    inverse_count = 1.0 / spec_count

    def correlate_group(group_values):
        return correlate(group_values.astype(jnp.float32), inverse_count)
    result = lax.map(correlate_group, grouped)
    return jnp.transpose(result, (1, 0, 2, 3, 4)).reshape(2, fft_len, input_count, input_count)
```

```python
import functools
import math

import jax
import jax.numpy as jnp
import numpy as np
from jax import lax
from jax.experimental import pallas as pl
from jax.experimental.pallas import tpu as pltpu
from jax.sharding import PartitionSpec as P

POLS = 2
LANES = 128
MESH = pl.DeviceIdType.MESH


def dft_halves(fft_len):
    index = np.arange(fft_len)
    phase_step = np.outer(index, index) % fft_len
    angles = phase_step * (2.0 * math.pi / fft_len)
    norm_scale = 1.0 / math.sqrt(fft_len)
    both = np.concatenate([np.cos(angles), np.sin(angles)], axis=1) * norm_scale
    return both.astype(np.float32).astype(jnp.bfloat16)


def kernel(
    blocks,
    halves,
    samples,
    history,
    coefficients,
    table,
    slot_station,
    station_ok,
    out,
    ext,
    wide,
    taps,
    cs,
    filt,
    fed,
    spectra,
    landed,
    turned,
    rotated,
    in_sem,
    tail_sem,
    send_sem,
    recv_sem,
):
    tap_count, fft_len = coefficients.shape
    rows = samples.shape[1]
    length = samples.shape[2]
    spec = length // fft_len
    past = history.shape[2]
    group = blocks * halves
    chans = fft_len // group
    parts = 2 * rows

    blk = lax.axis_index("blk")
    half = lax.axis_index("tch")
    me = blk * halves + half

    barrier = pltpu.get_barrier_semaphore()

    def greet(step, carry):
        other = lax.rem(me + step, group)
        pl.semaphore_signal(
            barrier,
            inc=1,
            device_id={"blk": other // halves, "tch": other % halves},
            device_id_type=MESH,
        )
        return carry

    lax.fori_loop(1, group, greet, 0)

    get_samples = pltpu.make_async_copy(samples, ext.at[:, :, pl.ds(past, length)], in_sem.at[0])
    get_taps = pltpu.make_async_copy(coefficients, taps, in_sem.at[1])
    get_table = pltpu.make_async_copy(table, cs, in_sem.at[2])
    get_history = pltpu.make_async_copy(history, ext.at[:, :, pl.ds(0, past)], in_sem.at[3])
    get_samples.start()
    get_taps.start()

    @pl.when(half == 0)
    def _():
        get_history.start()

    get_table.start()

    pl.semaphore_wait(barrier, group - 1)

    tail = pltpu.make_async_remote_copy(
        src_ref=samples.at[:, :, pl.ds(length - past, past)],
        dst_ref=ext.at[:, :, pl.ds(0, past)],
        send_sem=tail_sem.at[0],
        recv_sem=tail_sem.at[1],
        device_id={"tch": 1 - half},
        device_id_type=MESH,
    )

    @pl.when(half == 0)
    def _():
        tail.start()

    def widen(first, count):
        def one(m, carry):
            at = pl.ds(pl.multiple_of((first + m) * fft_len, fft_len), fft_len)
            wide[first + m, 0:rows, :] = ext[0, :, at].astype(jnp.float32)
            wide[first + m, rows:parts, :] = ext[1, :, at].astype(jnp.float32)
            return carry

        lax.fori_loop(0, count, one, 0)

    def filter_from(first, count):
        def lane_tile(tile, carry):
            at = pl.ds(pl.multiple_of(tile * LANES, LANES), LANES)
            weight = [
                jnp.broadcast_to(taps[j : j + 1, at], (parts, LANES)) for j in range(tap_count)
            ]
            for base in range(first, first + count, 8):
                sums = [None] * 8
                for m in range(8 + tap_count - 1):
                    block = wide[base + m, :, at]
                    for q in range(8):
                        j = m - q
                        if 0 <= j < tap_count:
                            term = weight[j] * block
                            sums[q] = term if j == 0 else sums[q] + term
                for q in range(8):
                    filt[pl.ds(tile * parts * spec + base + q, parts, stride=spec), :] = sums[q]
            return carry

        lax.fori_loop(0, fft_len // LANES, lane_tile, 0)

    early = tap_count
    get_samples.wait()
    get_taps.wait()
    widen(tap_count - 1, spec)
    filter_from(early, spec - early)

    @pl.when(half == 0)
    def _():
        get_history.wait()

    @pl.when(half == 1)
    def _():
        tail.wait_recv()

    widen(0, tap_count - 1)
    filter_from(0, early)

    def feed(tile, carry):
        left = pl.ds(pl.multiple_of(tile * LANES, LANES), LANES)
        right = pl.ds(pl.multiple_of(fft_len + tile * LANES, LANES), LANES)
        base = tile * parts * spec
        for a in range(rows):
            real_at = pl.ds(pl.multiple_of(base + a * spec, spec), spec)
            imag_at = pl.ds(pl.multiple_of(base + (rows + a) * spec, spec), spec)
            real = filt[real_at, :].astype(jnp.bfloat16)
            imag = filt[imag_at, :].astype(jnp.bfloat16)
            top = a * 2 * spec
            fed[top : top + spec, left] = real
            fed[top + spec : top + 2 * spec, left] = imag
            fed[top : top + spec, right] = imag
            fed[top + spec : top + 2 * spec, right] = -real
        return carry

    lax.fori_loop(0, fft_len // LANES, feed, 0)

    def piece(device):
        return spectra.at[:, pl.ds(pl.multiple_of(device * chans, chans), chans), :]

    def push(device):
        return pltpu.make_async_remote_copy(
            src_ref=piece(device),
            dst_ref=landed.at[me],
            send_sem=send_sem.at[device],
            recv_sem=recv_sem.at[me],
            device_id={"blk": device // halves, "tch": device % halves},
            device_id_type=MESH,
        )

    quarter = fft_len // 4
    per = group // 4
    mine = me // per
    get_table.wait()

    def channels_of(step):
        where = lax.rem(mine + 2, 4)
        beside = where + 1 - 2 * lax.rem(where, 2)
        near = mine + 1 - 2 * lax.rem(mine, 2)
        return (where, beside, near, mine)[step]

    for step in range(4):
        chunk = channels_of(step)
        at = pl.ds(pl.multiple_of(chunk * quarter, quarter), quarter)
        result = lax.dot_general(
            cs[at, :], fed[...], (((1,), (1,)), ((), ())), preferred_element_type=jnp.float32
        ).astype(jnp.bfloat16)
        for j in range(rows // POLS):
            spectra[j, at, :] = result[:, j * LANES : (j + 1) * LANES]
        if step < 3:
            for i in range(per):
                push(chunk * per + i).start()
        else:
            for i in range(1, per):
                push(chunk * per + lax.rem(me + i, per)).start()
    own = pltpu.make_async_copy(piece(me), landed.at[me], in_sem.at[4])
    own.start()

    @pl.when(half == 0)
    def _():
        tail.wait_send()

    own.wait()

    def arrive(step, carry):
        other = lax.rem(me + step, group)
        pltpu.make_async_remote_copy(
            src_ref=piece(other),
            dst_ref=landed.at[other],
            send_sem=send_sem.at[other],
            recv_sem=recv_sem.at[other],
            device_id={"blk": other // halves, "tch": other % halves},
            device_id_type=MESH,
        ).wait()
        return carry

    lax.fori_loop(1, group, arrive, 0)

    stations = slot_station.shape[0]
    inputs = stations * POLS
    lane = lax.broadcasted_iota(jnp.int32, (chans, LANES), 1)
    low = lane < LANES // 2
    real_lane = lax.rem(lane, LANES // 2) < LANES // 4

    def order(s, carry):
        slot = jnp.int32(0)
        for q in range(stations):
            slot = jnp.where(slot_station[q] == s, q, slot)
        source = lax.div(slot, rows // POLS)
        within = lax.rem(slot, rows // POLS)
        keep = station_ok[s].astype(jnp.float32)
        first = landed[source * halves, within].astype(jnp.float32) * keep
        second = landed[source * halves + 1, within].astype(jnp.float32) * keep
        one = jnp.where(low, first, pltpu.roll(second, LANES // 2, 1))
        two = jnp.where(low, pltpu.roll(first, LANES // 2, 1), second)
        for p, value in enumerate((one, two)):
            turn = jnp.where(
                real_lane,
                -pltpu.roll(value, LANES - LANES // 4, 1),
                pltpu.roll(value, LANES // 4, 1),
            )
            at = pl.ds(s * POLS + p, chans, stride=inputs)
            turned[at, :] = value
            rotated[at, :] = turn
        return carry

    lax.fori_loop(0, stations, order, 0)

    scale = 1.0 / (spec * halves)
    unroll = 8

    def correlate(step, carry):
        for i in range(unroll):
            c = step * unroll + i
            at = pl.ds(pl.multiple_of(c * inputs, inputs), inputs)
            y = turned[at, :].astype(jnp.bfloat16)
            z = rotated[at, :].astype(jnp.bfloat16)
            for part, other in ((0, y), (1, z)):
                vis = lax.dot_general(
                    y, other, (((1,), (1,)), ((), ())), preferred_element_type=jnp.float32
                )
                out[part, c] = (vis * scale).astype(jnp.bfloat16)
        return carry

    lax.fori_loop(0, chans // unroll, correlate, 0)


def in_one_kernel(samples, history, coefficients, station_of_slot, station_ok):
    tap_count, fft_len = coefficients.shape
    rows = samples.shape[1]
    spec = samples.shape[2] // fft_len
    halves = lax.axis_size("tch")
    blocks = lax.axis_size("blk")
    group = blocks * halves
    chans = fft_len // group
    inputs = blocks * rows
    parts = 2 * rows
    table = jnp.asarray(dft_halves(fft_len))
    anywhere = pl.BlockSpec(memory_space=pl.ANY)
    scalars = pl.BlockSpec(memory_space=pltpu.SMEM)
    return pl.pallas_call(
        functools.partial(kernel, blocks, halves),
        out_shape=jax.ShapeDtypeStruct((2, chans, inputs, inputs), jnp.bfloat16),
        in_specs=[anywhere] * 4 + [scalars] * 2,
        out_specs=pl.BlockSpec(memory_space=pltpu.VMEM),
        scratch_shapes=[
            pltpu.VMEM((2, rows, history.shape[2] + samples.shape[2]), jnp.bfloat16),
            pltpu.VMEM((tap_count - 1 + spec, parts, fft_len), jnp.float32),
            pltpu.VMEM((tap_count, fft_len), jnp.float32),
            pltpu.VMEM((fft_len, 2 * fft_len), jnp.bfloat16),
            pltpu.VMEM((fft_len // LANES * parts * spec, LANES), jnp.float32),
            pltpu.VMEM((parts * spec, 2 * fft_len), jnp.bfloat16),
            pltpu.VMEM((rows // POLS, fft_len, LANES), jnp.bfloat16),
            pltpu.VMEM((group, rows // POLS, chans, LANES), jnp.bfloat16),
            pltpu.VMEM((chans * inputs, LANES), jnp.float32),
            pltpu.VMEM((chans * inputs, LANES), jnp.float32),
            pltpu.SemaphoreType.DMA((5,)),
            pltpu.SemaphoreType.DMA((2,)),
            pltpu.SemaphoreType.DMA((group,)),
            pltpu.SemaphoreType.DMA((group,)),
        ],
        compiler_params=pltpu.CompilerParams(
            collective_id=0, has_side_effects=True, vmem_limit_bytes=62 * 2**20
        ),
    )(samples, history, coefficients, table, station_of_slot, station_ok)


def filter_bank(extended, coefficients, spec_count):
    tap_count, fft_len = coefficients.shape
    blocks = extended.reshape(extended.shape[0], extended.shape[1], -1, fft_len)
    running = jnp.zeros((extended.shape[0], extended.shape[1], spec_count, fft_len), jnp.float32)
    for j in range(tap_count):
        running = running + coefficients[j] * blocks[:, :, j : j + spec_count, :].astype(jnp.float32)
    return running.astype(jnp.bfloat16)


def in_parts(samples, history, coefficients, station_of_slot, station_ok):
    tap_count, fft_len = coefficients.shape
    rows = samples.shape[1]
    spec = samples.shape[2] // fft_len
    halves = lax.axis_size("tch")
    blocks = lax.axis_size("blk")
    inputs = blocks * rows
    total = spec * halves
    past = (tap_count - 1) * fft_len
    ends = jnp.concatenate([history, samples], axis=2)[:, :, -past:]
    earlier = lax.ppermute(ends, "tch", [(i, i + 1) for i in range(halves - 1)])
    earlier = jnp.where(lax.axis_index("tch") == 0, history, earlier)
    filtered = filter_bank(jnp.concatenate([earlier, samples], axis=2), coefficients, spec)
    both = jnp.asarray(dft_halves(fft_len))
    cosine, sine = both[:, :fft_len], both[:, fft_len:]
    matrix = jnp.concatenate(
        [jnp.concatenate([cosine, -sine], axis=1), jnp.concatenate([sine, cosine], axis=1)], axis=0
    )
    flat = jnp.transpose(filtered, (1, 2, 0, 3)).reshape(rows * spec, 2 * fft_len)
    product = jnp.dot(flat, matrix, preferred_element_type=jnp.float32).astype(jnp.bfloat16)
    product = product.reshape(rows, spec, 2, fft_len)
    major = jnp.transpose(product, (3, 0, 2, 1)).reshape(fft_len, rows * 2 * spec)
    major = lax.all_to_all(major, "blk", split_axis=0, concat_axis=1, tiled=True)
    major = lax.all_to_all(major, "tch", split_axis=0, concat_axis=1, tiled=True)
    chans = major.shape[0]
    layout = major.reshape(chans, halves, blocks, rows, 2, spec)
    stacked = jnp.transpose(layout, (0, 2, 3, 4, 1, 5)).reshape(chans, inputs, 2 * total)
    target = jnp.arange(inputs, dtype=jnp.int32)
    station_in = jnp.repeat(station_of_slot, POLS) * POLS + target % POLS
    choose = (target[:, None] == station_in[None, :]) & (jnp.repeat(station_ok, POLS) == 1)[:, None]
    ordered = jnp.einsum(
        "ab,cbk->cak", choose.astype(jnp.bfloat16), stacked, preferred_element_type=jnp.float32
    ).astype(jnp.bfloat16)
    turn = jnp.concatenate([-ordered[:, :, total:], ordered[:, :, :total]], axis=2)
    real = jnp.einsum("cak,cbk->cab", ordered, ordered, preferred_element_type=jnp.float32)
    imag = jnp.einsum("cak,cbk->cab", ordered, turn, preferred_element_type=jnp.float32)
    return (jnp.stack([real, imag], axis=0) * (1.0 / total)).astype(jnp.bfloat16)


def local(samples, history, coefficients, station_of_slot, station_ok):
    tap_count, fft_len = coefficients.shape
    rows = samples.shape[1]
    spec = samples.shape[2] // fft_len
    halves = lax.axis_size("tch")
    group = lax.axis_size("blk") * halves
    chans = fft_len // group
    fits = (
        halves == 2
        and group % 4 == 0
        and chans % 16 == 0
        and rows % POLS == 0
        and 2 * rows == 8
        and POLS * 2 * spec == LANES
        and tap_count <= spec
        and tap_count % 8 == 0
    )
    form = in_one_kernel if fits else in_parts
    return form(samples, history, coefficients, station_of_slot, station_ok)


def solution(mesh):
    return jax.shard_map(
        local,
        mesh=mesh,
        in_specs=(P("grp", "blk", "tch"), P("grp", "blk", None), P(), P("grp"), P("grp")),
        out_specs=P("grp", ("blk", "tch"), None, None),
        check_vma=False,
    )
```

```python
import functools
import math

import jax
import jax.numpy as jnp
import numpy as np
from jax import lax
from jax.experimental import pallas as pl
from jax.experimental.pallas import tpu as pltpu
from jax.sharding import PartitionSpec as P

POLS = 2
LANES = 128
MESH = pl.DeviceIdType.MESH


def dft_halves(fft_len):
    index = np.arange(fft_len)
    phase_step = np.outer(index, index) % fft_len
    angles = phase_step * (2.0 * math.pi / fft_len)
    norm_scale = 1.0 / math.sqrt(fft_len)
    both = np.concatenate([np.cos(angles), np.sin(angles)], axis=1) * norm_scale
    return both.astype(np.float32).astype(jnp.bfloat16)


def kernel(
    blocks,
    halves,
    samples,
    history,
    coefficients,
    table,
    slot_station,
    station_ok,
    out,
    ext,
    wide,
    taps,
    cs,
    filt,
    fed,
    spectra,
    landed,
    turned,
    planes,
    in_sem,
    tail_sem,
    send_sem,
    recv_sem,
):
    tap_count, fft_len = coefficients.shape
    rows = samples.shape[1]
    length = samples.shape[2]
    spec = length // fft_len
    past = history.shape[2]
    group = blocks * halves
    chans = fft_len // group
    parts = 2 * rows

    blk = lax.axis_index("blk")
    half = lax.axis_index("tch")
    me = blk * halves + half

    barrier = pltpu.get_barrier_semaphore()

    def greet(step, carry):
        other = lax.rem(me + step, group)
        pl.semaphore_signal(
            barrier,
            inc=1,
            device_id={"blk": other // halves, "tch": other % halves},
            device_id_type=MESH,
        )
        return carry

    lax.fori_loop(1, group, greet, 0)

    get_samples = pltpu.make_async_copy(samples, ext.at[:, :, pl.ds(past, length)], in_sem.at[0])
    get_taps = pltpu.make_async_copy(coefficients, taps, in_sem.at[1])
    get_table = pltpu.make_async_copy(table, cs, in_sem.at[2])
    get_history = pltpu.make_async_copy(history, ext.at[:, :, pl.ds(0, past)], in_sem.at[3])
    get_samples.start()
    get_taps.start()

    @pl.when(half == 0)
    def _():
        get_history.start()

    get_table.start()

    pl.semaphore_wait(barrier, group - 1)

    planes[...] = jnp.zeros_like(planes)

    tail = pltpu.make_async_remote_copy(
        src_ref=samples.at[:, :, pl.ds(length - past, past)],
        dst_ref=ext.at[:, :, pl.ds(0, past)],
        send_sem=tail_sem.at[0],
        recv_sem=tail_sem.at[1],
        device_id={"tch": 1 - half},
        device_id_type=MESH,
    )

    @pl.when(half == 0)
    def _():
        tail.start()

    def widen(first, count):
        def one(m, carry):
            at = pl.ds(pl.multiple_of((first + m) * fft_len, fft_len), fft_len)
            wide[first + m, 0:rows, :] = ext[0, :, at].astype(jnp.float32)
            wide[first + m, rows:parts, :] = ext[1, :, at].astype(jnp.float32)
            return carry

        lax.fori_loop(0, count, one, 0)

    def filter_from(first, count):
        def lane_tile(tile, carry):
            at = pl.ds(pl.multiple_of(tile * LANES, LANES), LANES)
            weight = [
                jnp.broadcast_to(taps[j : j + 1, at], (parts, LANES)) for j in range(tap_count)
            ]
            for base in range(first, first + count, 8):
                sums = [None] * 8
                for m in range(8 + tap_count - 1):
                    block = wide[base + m, :, at]
                    for q in range(8):
                        j = m - q
                        if 0 <= j < tap_count:
                            term = weight[j] * block
                            sums[q] = term if j == 0 else sums[q] + term
                for q in range(8):
                    filt[pl.ds(tile * parts * spec + base + q, parts, stride=spec), :] = sums[q]
            return carry

        lax.fori_loop(0, fft_len // LANES, lane_tile, 0)

    early = tap_count
    get_samples.wait()
    get_taps.wait()
    widen(tap_count - 1, spec)
    filter_from(early, spec - early)

    @pl.when(half == 0)
    def _():
        get_history.wait()

    @pl.when(half == 1)
    def _():
        tail.wait_recv()

    widen(0, tap_count - 1)
    filter_from(0, early)

    def feed(tile, carry):
        left = pl.ds(pl.multiple_of(tile * LANES, LANES), LANES)
        right = pl.ds(pl.multiple_of(fft_len + tile * LANES, LANES), LANES)
        base = tile * parts * spec
        for a in range(rows):
            real_at = pl.ds(pl.multiple_of(base + a * spec, spec), spec)
            imag_at = pl.ds(pl.multiple_of(base + (rows + a) * spec, spec), spec)
            real = filt[real_at, :].astype(jnp.bfloat16)
            imag = filt[imag_at, :].astype(jnp.bfloat16)
            top = a * 2 * spec
            fed[top : top + spec, left] = real
            fed[top + spec : top + 2 * spec, left] = imag
            fed[top : top + spec, right] = imag
            fed[top + spec : top + 2 * spec, right] = -real
        return carry

    lax.fori_loop(0, fft_len // LANES, feed, 0)

    def piece(device):
        return spectra.at[:, pl.ds(pl.multiple_of(device * chans, chans), chans), :]

    def push(device):
        return pltpu.make_async_remote_copy(
            src_ref=piece(device),
            dst_ref=landed.at[me],
            send_sem=send_sem.at[device],
            recv_sem=recv_sem.at[me],
            device_id={"blk": device // halves, "tch": device % halves},
            device_id_type=MESH,
        )

    quarter = fft_len // 4
    per = group // 4
    mine = me // per
    get_table.wait()

    def channels_of(step):
        where = lax.rem(mine + 2, 4)
        beside = where + 1 - 2 * lax.rem(where, 2)
        near = mine + 1 - 2 * lax.rem(mine, 2)
        return (where, beside, near, mine)[step]

    for step in range(4):
        chunk = channels_of(step)
        at = pl.ds(pl.multiple_of(chunk * quarter, quarter), quarter)
        result = lax.dot_general(
            cs[at, :], fed[...], (((1,), (1,)), ((), ())), preferred_element_type=jnp.float32
        ).astype(jnp.bfloat16)
        for j in range(rows // POLS):
            spectra[j, at, :] = result[:, j * LANES : (j + 1) * LANES]
        if step < 3:
            for i in range(per):
                push(chunk * per + i).start()
        else:
            for i in range(1, per):
                push(chunk * per + lax.rem(me + i, per)).start()
    own = pltpu.make_async_copy(piece(me), landed.at[me], in_sem.at[4])
    own.start()

    @pl.when(half == 0)
    def _():
        tail.wait_send()

    own.wait()

    def arrive(step, carry):
        other = lax.rem(me + step, group)
        pltpu.make_async_remote_copy(
            src_ref=piece(other),
            dst_ref=landed.at[other],
            send_sem=send_sem.at[other],
            recv_sem=recv_sem.at[other],
            device_id={"blk": other // halves, "tch": other % halves},
            device_id_type=MESH,
        ).wait()
        return carry

    lax.fori_loop(1, group, arrive, 0)

    stations = slot_station.shape[0]
    inputs = stations * POLS
    lane = lax.broadcasted_iota(jnp.int32, (chans, LANES), 1)
    low = lane < LANES // 2
    real_lane = lax.rem(lane, LANES // 2) < LANES // 4

    def order(s, carry):
        slot = jnp.int32(0)
        for q in range(stations):
            slot = jnp.where(slot_station[q] == s, q, slot)
        source = lax.div(slot, rows // POLS)
        within = lax.rem(slot, rows // POLS)
        keep = station_ok[s].astype(jnp.float32)
        first = landed[source * halves, within].astype(jnp.float32) * keep
        second = landed[source * halves + 1, within].astype(jnp.float32) * keep
        one = jnp.where(low, first, pltpu.roll(second, LANES // 2, 1))
        two = jnp.where(low, pltpu.roll(first, LANES // 2, 1), second)
        for p, value in enumerate((one, two)):
            turn = jnp.where(
                real_lane,
                -pltpu.roll(value, LANES - LANES // 4, 1),
                pltpu.roll(value, LANES // 4, 1),
            )
            turned[pl.ds(s * POLS + p, chans, stride=2 * inputs), :] = value
            turned[pl.ds(inputs + s * POLS + p, chans, stride=2 * inputs), :] = turn
        return carry

    lax.fori_loop(0, stations, order, 0)

    scale = 1.0 / (spec * halves)
    unroll = 8

    def correlate(step, carry):
        for i in range(unroll):
            c = step * unroll + i
            at = pl.ds(pl.multiple_of(c * 2 * inputs, 2 * inputs), 2 * inputs)
            both = turned[at, :].astype(jnp.bfloat16)
            planes[pl.ds(pl.multiple_of(c * inputs, inputs), inputs), 0 : 2 * inputs] = (
                lax.dot_general(
                    both[0:inputs, :],
                    both,
                    (((1,), (1,)), ((), ())),
                    preferred_element_type=jnp.float32,
                )
            )
        return carry

    lax.fori_loop(0, chans // unroll, correlate, 0)

    def lay_out(step, carry):
        for i in range(4):
            a = step * 4 + i
            vis = jnp.transpose(planes[pl.ds(a, chans, stride=inputs), :] * scale)
            out[0, a] = vis[0:inputs, :].astype(jnp.bfloat16)
            out[1, a] = vis[inputs : 2 * inputs, :].astype(jnp.bfloat16)
        return carry

    lax.fori_loop(0, inputs // 4, lay_out, 0)


def in_one_kernel(samples, history, coefficients, station_of_slot, station_ok):
    tap_count, fft_len = coefficients.shape
    rows = samples.shape[1]
    spec = samples.shape[2] // fft_len
    halves = lax.axis_size("tch")
    blocks = lax.axis_size("blk")
    group = blocks * halves
    chans = fft_len // group
    inputs = blocks * rows
    parts = 2 * rows
    table = jnp.asarray(dft_halves(fft_len))
    anywhere = pl.BlockSpec(memory_space=pl.ANY)
    scalars = pl.BlockSpec(memory_space=pltpu.SMEM)
    visibilities = pl.pallas_call(
        functools.partial(kernel, blocks, halves),
        out_shape=jax.ShapeDtypeStruct((2, inputs, inputs, chans), jnp.bfloat16),
        in_specs=[anywhere] * 4 + [scalars] * 2,
        out_specs=pl.BlockSpec(memory_space=pltpu.VMEM),
        scratch_shapes=[
            pltpu.VMEM((2, rows, history.shape[2] + samples.shape[2]), jnp.bfloat16),
            pltpu.VMEM((tap_count - 1 + spec, parts, fft_len), jnp.float32),
            pltpu.VMEM((tap_count, fft_len), jnp.float32),
            pltpu.VMEM((fft_len, 2 * fft_len), jnp.bfloat16),
            pltpu.VMEM((fft_len // LANES * parts * spec, LANES), jnp.float32),
            pltpu.VMEM((parts * spec, 2 * fft_len), jnp.bfloat16),
            pltpu.VMEM((rows // POLS, fft_len, LANES), jnp.bfloat16),
            pltpu.VMEM((group, rows // POLS, chans, LANES), jnp.bfloat16),
            pltpu.VMEM((chans * 2 * inputs, LANES), jnp.float32),
            pltpu.VMEM((chans * inputs, LANES), jnp.float32),
            pltpu.SemaphoreType.DMA((5,)),
            pltpu.SemaphoreType.DMA((2,)),
            pltpu.SemaphoreType.DMA((group,)),
            pltpu.SemaphoreType.DMA((group,)),
        ],
        compiler_params=pltpu.CompilerParams(
            collective_id=0, has_side_effects=True, vmem_limit_bytes=62 * 2**20
        ),
    )(samples, history, coefficients, table, station_of_slot, station_ok)
    return jnp.transpose(visibilities, (0, 3, 1, 2))


def filter_bank(extended, coefficients, spec_count):
    tap_count, fft_len = coefficients.shape
    blocks = extended.reshape(extended.shape[0], extended.shape[1], -1, fft_len)
    running = jnp.zeros((extended.shape[0], extended.shape[1], spec_count, fft_len), jnp.float32)
    for j in range(tap_count):
        running = running + coefficients[j] * blocks[:, :, j : j + spec_count, :].astype(jnp.float32)
    return running.astype(jnp.bfloat16)


def in_parts(samples, history, coefficients, station_of_slot, station_ok):
    tap_count, fft_len = coefficients.shape
    rows = samples.shape[1]
    spec = samples.shape[2] // fft_len
    halves = lax.axis_size("tch")
    blocks = lax.axis_size("blk")
    inputs = blocks * rows
    total = spec * halves
    past = (tap_count - 1) * fft_len
    ends = jnp.concatenate([history, samples], axis=2)[:, :, -past:]
    earlier = lax.ppermute(ends, "tch", [(i, i + 1) for i in range(halves - 1)])
    earlier = jnp.where(lax.axis_index("tch") == 0, history, earlier)
    filtered = filter_bank(jnp.concatenate([earlier, samples], axis=2), coefficients, spec)
    both = jnp.asarray(dft_halves(fft_len))
    cosine, sine = both[:, :fft_len], both[:, fft_len:]
    matrix = jnp.concatenate(
        [jnp.concatenate([cosine, -sine], axis=1), jnp.concatenate([sine, cosine], axis=1)], axis=0
    )
    flat = jnp.transpose(filtered, (1, 2, 0, 3)).reshape(rows * spec, 2 * fft_len)
    product = jnp.dot(flat, matrix, preferred_element_type=jnp.float32).astype(jnp.bfloat16)
    product = product.reshape(rows, spec, 2, fft_len)
    major = jnp.transpose(product, (3, 0, 2, 1)).reshape(fft_len, rows * 2 * spec)
    major = lax.all_to_all(major, "blk", split_axis=0, concat_axis=1, tiled=True)
    major = lax.all_to_all(major, "tch", split_axis=0, concat_axis=1, tiled=True)
    chans = major.shape[0]
    layout = major.reshape(chans, halves, blocks, rows, 2, spec)
    stacked = jnp.transpose(layout, (0, 2, 3, 4, 1, 5)).reshape(chans, inputs, 2 * total)
    target = jnp.arange(inputs, dtype=jnp.int32)
    station_in = jnp.repeat(station_of_slot, POLS) * POLS + target % POLS
    choose = (target[:, None] == station_in[None, :]) & (jnp.repeat(station_ok, POLS) == 1)[:, None]
    ordered = jnp.einsum(
        "ab,cbk->cak", choose.astype(jnp.bfloat16), stacked, preferred_element_type=jnp.float32
    ).astype(jnp.bfloat16)
    turn = jnp.concatenate([-ordered[:, :, total:], ordered[:, :, :total]], axis=2)
    real = jnp.einsum("cak,cbk->cab", ordered, ordered, preferred_element_type=jnp.float32)
    imag = jnp.einsum("cak,cbk->cab", ordered, turn, preferred_element_type=jnp.float32)
    return (jnp.stack([real, imag], axis=0) * (1.0 / total)).astype(jnp.bfloat16)


def local(samples, history, coefficients, station_of_slot, station_ok):
    tap_count, fft_len = coefficients.shape
    rows = samples.shape[1]
    spec = samples.shape[2] // fft_len
    halves = lax.axis_size("tch")
    blocks = lax.axis_size("blk")
    group = blocks * halves
    chans = fft_len // group
    fits = (
        halves == 2
        and group % 4 == 0
        and chans % 16 == 0
        and rows % POLS == 0
        and 2 * blocks * rows <= LANES
        and 2 * rows == 8
        and POLS * 2 * spec == LANES
        and tap_count <= spec
        and tap_count % 8 == 0
    )
    form = in_one_kernel if fits else in_parts
    return form(samples, history, coefficients, station_of_slot, station_ok)


def solution(mesh):
    return jax.shard_map(
        local,
        mesh=mesh,
        in_specs=(P("grp", "blk", "tch"), P("grp", "blk", None), P(), P("grp"), P("grp")),
        out_specs=P("grp", ("blk", "tch"), None, None),
        check_vma=False,
    )
```

```python
import functools
import math

import jax
import jax.numpy as jnp
import numpy as np
from jax import lax
from jax.experimental import pallas as pl
from jax.experimental.pallas import tpu as pltpu
from jax.sharding import PartitionSpec as P

POLS = 2
ROUNDS = 4
PAD = 8
LANES = 128
MESH = pl.DeviceIdType.MESH


def by_round(table, group, rounds):
    fft_len = table.shape[0]
    return (
        table.reshape(group, rounds, fft_len // group // rounds, -1)
        .transpose(1, 0, 2, 3)
        .reshape(fft_len, -1)
    )


def dft_halves(fft_len):
    index = np.arange(fft_len)
    phase_step = np.outer(index, index) % fft_len
    angles = phase_step * (2.0 * math.pi / fft_len)
    norm_scale = 1.0 / math.sqrt(fft_len)
    both = np.concatenate([np.cos(angles), np.sin(angles)], axis=1) * norm_scale
    return both.astype(np.float32).astype(jnp.bfloat16)


def kernel(
    blocks,
    halves,
    samples,
    history,
    coefficients,
    table,
    slot_station,
    station_ok,
    out,
    ext,
    wide,
    taps,
    cs,
    filt,
    fed,
    spectra,
    *rest,
):
    landed = rest[:ROUNDS]
    turned, planes, slots, in_sem, own_sem, tail_sem, send_sem, recv_sem = rest[ROUNDS:]
    tap_count, fft_len = coefficients.shape
    rows = samples.shape[1]
    length = samples.shape[2]
    spec = length // fft_len
    past = history.shape[2]
    group = blocks * halves
    chans = fft_len // group
    sub = chans // ROUNDS
    parts = 2 * rows
    pitch = spec + PAD
    stations = slot_station.shape[0]
    inputs = stations * POLS
    deep = 2 * inputs + PAD
    flat = inputs + PAD

    blk = lax.axis_index("blk")
    half = lax.axis_index("tch")
    me = blk * halves + half

    barrier = pltpu.get_barrier_semaphore()

    def greet(step, carry):
        other = lax.rem(me + step, group)
        pl.semaphore_signal(
            barrier,
            inc=1,
            device_id={"blk": other // halves, "tch": other % halves},
            device_id_type=MESH,
        )
        return carry

    lax.fori_loop(1, group, greet, 0)

    get_samples = pltpu.make_async_copy(samples, ext.at[:, :, pl.ds(past, length)], in_sem.at[0])
    get_taps = pltpu.make_async_copy(coefficients, taps, in_sem.at[1])
    get_table = pltpu.make_async_copy(table, cs, in_sem.at[2])
    get_history = pltpu.make_async_copy(history, ext.at[:, :, pl.ds(0, past)], in_sem.at[3])
    get_samples.start()
    get_taps.start()

    @pl.when(half == 0)
    def _():
        get_history.start()

    get_table.start()

    pl.semaphore_wait(barrier, group - 1)

    planes[...] = jnp.zeros_like(planes)

    tail = pltpu.make_async_remote_copy(
        src_ref=samples.at[:, :, pl.ds(length - past, past)],
        dst_ref=ext.at[:, :, pl.ds(0, past)],
        send_sem=tail_sem.at[0],
        recv_sem=tail_sem.at[1],
        device_id={"tch": 1 - half},
        device_id_type=MESH,
    )

    @pl.when(half == 0)
    def _():
        tail.start()

    def widen(first, count):
        def one(m, carry):
            at = pl.ds(pl.multiple_of((first + m) * fft_len, fft_len), fft_len)
            wide[first + m, 0:rows, :] = ext[0, :, at].astype(jnp.float32)
            wide[first + m, rows:parts, :] = ext[1, :, at].astype(jnp.float32)
            return carry

        lax.fori_loop(0, count, one, 0)

    def filter_from(first, count):
        def lane_tile(tile, carry):
            at = pl.ds(pl.multiple_of(tile * LANES, LANES), LANES)
            weight = [
                jnp.broadcast_to(taps[j : j + 1, at], (parts, LANES)) for j in range(tap_count)
            ]
            for base in range(first, first + count, 8):
                sums = [None] * 8
                for m in range(8 + tap_count - 1):
                    block = wide[base + m, :, at]
                    for q in range(8):
                        j = m - q
                        if 0 <= j < tap_count:
                            term = weight[j] * block
                            sums[q] = term if j == 0 else sums[q] + term
                for q in range(8):
                    filt[pl.ds(tile * parts * pitch + base + q, parts, stride=pitch), :] = sums[q]
            return carry

        lax.fori_loop(0, fft_len // LANES, lane_tile, 0)

    early = tap_count
    get_samples.wait()
    get_taps.wait()
    widen(tap_count - 1, spec)
    filter_from(early, spec - early)

    @pl.when(half == 0)
    def _():
        get_history.wait()

    @pl.when(half == 1)
    def _():
        tail.wait_recv()

    widen(0, tap_count - 1)
    filter_from(0, early)

    def feed(tile, carry):
        left = pl.ds(pl.multiple_of(tile * LANES, LANES), LANES)
        right = pl.ds(pl.multiple_of(fft_len + tile * LANES, LANES), LANES)
        base = tile * parts * pitch
        for a in range(rows):
            real_at = pl.ds(pl.multiple_of(base + a * pitch, 8), spec)
            imag_at = pl.ds(pl.multiple_of(base + (rows + a) * pitch, 8), spec)
            real = filt[real_at, :].astype(jnp.bfloat16)
            imag = filt[imag_at, :].astype(jnp.bfloat16)
            top = a * 2 * spec
            fed[top : top + spec, left] = real
            fed[top + spec : top + 2 * spec, left] = imag
            fed[top : top + spec, right] = imag
            fed[top + spec : top + 2 * spec, right] = -real
        return carry

    lax.fori_loop(0, fft_len // LANES, feed, 0)

    def part_of(turn, device):
        first = (turn * group + device) * sub
        return spectra.at[:, pl.ds(pl.multiple_of(first, sub), sub), :]

    def push(turn, device):
        return pltpu.make_async_remote_copy(
            src_ref=part_of(turn, device),
            dst_ref=landed[turn].at[me],
            send_sem=send_sem.at[turn, device],
            recv_sem=recv_sem.at[turn, me],
            device_id={"blk": device // halves, "tch": device % halves},
            device_id_type=MESH,
        )

    per = group // 4
    mine = me // per
    across = lax.rem(mine + 2, 4)
    beside = across + 1 - 2 * lax.rem(across, 2)
    near = mine + 1 - 2 * lax.rem(mine, 2)
    block = fft_len // ROUNDS
    get_table.wait()

    for turn in range(ROUNDS):
        at = slice(turn * block, (turn + 1) * block)
        result = lax.dot_general(
            cs[at, :], fed[...], (((1,), (1,)), ((), ())), preferred_element_type=jnp.float32
        ).astype(jnp.bfloat16)
        for j in range(rows // POLS):
            spectra[j, at, :] = result[:, j * LANES : (j + 1) * LANES]
        for chunk in (across, beside, near):
            for i in range(per):
                push(turn, chunk * per + lax.rem(me + i, per)).start()
        for i in range(1, per):
            push(turn, mine * per + lax.rem(me + i, per)).start()
        pltpu.make_async_copy(part_of(turn, me), landed[turn].at[me], own_sem.at[turn]).start()

    for s in range(stations):
        slot = jnp.int32(0)
        for q in range(stations):
            slot = jnp.where(slot_station[q] == s, q, slot)
        slots[s] = slot

    def arrival(turn, step):
        other = lax.rem(me + step, group)
        return pltpu.make_async_remote_copy(
            src_ref=part_of(turn, other),
            dst_ref=landed[turn].at[other],
            send_sem=send_sem.at[turn, other],
            recv_sem=recv_sem.at[turn, other],
            device_id={"blk": other // halves, "tch": other % halves},
            device_id_type=MESH,
        )

    lane = lax.broadcasted_iota(jnp.int32, (sub, LANES), 1)
    low = lane < LANES // 2
    real_lane = lax.rem(lane, LANES // 2) < LANES // 4

    def order(turn, s):
        slot = slots[s]
        source = lax.div(slot, rows // POLS)
        within = lax.rem(slot, rows // POLS)
        keep = station_ok[s].astype(jnp.float32)
        first = landed[turn][source * halves, within].astype(jnp.float32) * keep
        second = landed[turn][source * halves + 1, within].astype(jnp.float32) * keep
        one = jnp.where(low, first, pltpu.roll(second, LANES // 2, 1))
        two = jnp.where(low, pltpu.roll(first, LANES // 2, 1), second)
        for p, value in enumerate((one, two)):
            turned_value = jnp.where(
                real_lane,
                -pltpu.roll(value, LANES - LANES // 4, 1),
                pltpu.roll(value, LANES // 4, 1),
            )
            turned[pl.ds(s * POLS + p, sub, stride=deep), :] = value
            turned[pl.ds(inputs + s * POLS + p, sub, stride=deep), :] = turned_value

    scale = 1.0 / (spec * halves)

    def correlate(turn, c):
        both = turned[c * deep : c * deep + 2 * inputs, :].astype(jnp.bfloat16)
        first = (turn * sub + c) * flat
        planes[pl.ds(pl.multiple_of(first, 8), inputs), 0 : 2 * inputs] = lax.dot_general(
            both[0:inputs, :], both, (((1,), (1,)), ((), ())), preferred_element_type=jnp.float32
        )

    def finish(turn):
        def arrive(step, inner):
            arrival(turn, step).wait_recv()
            return inner

        lax.fori_loop(1, group, arrive, 0)
        pltpu.make_async_copy(part_of(turn, me), landed[turn].at[me], own_sem.at[turn]).wait()
        for s in range(stations):
            order(turn, s)
        for c in range(sub):
            correlate(turn, c)

    for turn in range(ROUNDS):
        finish(turn)

    def lay_out(step, carry):
        for i in range(4):
            a = step * 4 + i
            vis = jnp.transpose(planes[pl.ds(a, chans, stride=flat), :] * scale)
            out[0, a] = vis[0:inputs, :].astype(jnp.bfloat16)
            out[1, a] = vis[inputs : 2 * inputs, :].astype(jnp.bfloat16)
        return carry

    lax.fori_loop(0, inputs // 4, lay_out, 0)

    @pl.when(half == 0)
    def _():
        tail.wait_send()

    for turn in range(ROUNDS):

        def sent(step, carry, turn=turn):
            arrival(turn, step).wait_send()
            return carry

        lax.fori_loop(1, group, sent, 0)


def in_one_kernel(samples, history, coefficients, station_of_slot, station_ok):
    tap_count, fft_len = coefficients.shape
    rows = samples.shape[1]
    spec = samples.shape[2] // fft_len
    halves = lax.axis_size("tch")
    blocks = lax.axis_size("blk")
    group = blocks * halves
    chans = fft_len // group
    inputs = blocks * rows
    parts = 2 * rows
    table = jnp.asarray(by_round(dft_halves(fft_len), group, ROUNDS))
    sub = chans // ROUNDS
    anywhere = pl.BlockSpec(memory_space=pl.ANY)
    scalars = pl.BlockSpec(memory_space=pltpu.SMEM)
    visibilities = pl.pallas_call(
        functools.partial(kernel, blocks, halves),
        out_shape=jax.ShapeDtypeStruct((2, inputs, inputs, chans), jnp.bfloat16),
        in_specs=[anywhere] * 4 + [scalars] * 2,
        out_specs=pl.BlockSpec(memory_space=pltpu.VMEM),
        scratch_shapes=[
            pltpu.VMEM((2, rows, history.shape[2] + samples.shape[2]), jnp.bfloat16),
            pltpu.VMEM((tap_count - 1 + spec, parts, fft_len), jnp.float32),
            pltpu.VMEM((tap_count, fft_len), jnp.float32),
            pltpu.VMEM((fft_len, 2 * fft_len), jnp.bfloat16),
            pltpu.VMEM((fft_len // LANES * parts * (spec + PAD), LANES), jnp.float32),
            pltpu.VMEM((parts * spec, 2 * fft_len), jnp.bfloat16),
            pltpu.VMEM((rows // POLS, fft_len, LANES), jnp.bfloat16),
            *[pltpu.VMEM((group, rows // POLS, sub, LANES), jnp.bfloat16)] * ROUNDS,
            pltpu.VMEM((sub * (2 * inputs + PAD), LANES), jnp.float32),
            pltpu.VMEM((chans * (inputs + PAD), LANES), jnp.float32),
            pltpu.SMEM((inputs // POLS,), jnp.int32),
            pltpu.SemaphoreType.DMA((4,)),
            pltpu.SemaphoreType.DMA((ROUNDS,)),
            pltpu.SemaphoreType.DMA((2,)),
            pltpu.SemaphoreType.DMA((ROUNDS, group)),
            pltpu.SemaphoreType.DMA((ROUNDS, group)),
        ],
        compiler_params=pltpu.CompilerParams(
            collective_id=0, has_side_effects=True, vmem_limit_bytes=62 * 2**20
        ),
    )(samples, history, coefficients, table, station_of_slot, station_ok)
    return jnp.transpose(visibilities, (0, 3, 1, 2))


def filter_bank(extended, coefficients, spec_count):
    tap_count, fft_len = coefficients.shape
    blocks = extended.reshape(extended.shape[0], extended.shape[1], -1, fft_len)
    running = jnp.zeros((extended.shape[0], extended.shape[1], spec_count, fft_len), jnp.float32)
    for j in range(tap_count):
        running = running + coefficients[j] * blocks[:, :, j : j + spec_count, :].astype(jnp.float32)
    return running.astype(jnp.bfloat16)


def in_parts(samples, history, coefficients, station_of_slot, station_ok):
    tap_count, fft_len = coefficients.shape
    rows = samples.shape[1]
    spec = samples.shape[2] // fft_len
    halves = lax.axis_size("tch")
    blocks = lax.axis_size("blk")
    inputs = blocks * rows
    total = spec * halves
    past = (tap_count - 1) * fft_len
    ends = jnp.concatenate([history, samples], axis=2)[:, :, -past:]
    earlier = lax.ppermute(ends, "tch", [(i, i + 1) for i in range(halves - 1)])
    earlier = jnp.where(lax.axis_index("tch") == 0, history, earlier)
    filtered = filter_bank(jnp.concatenate([earlier, samples], axis=2), coefficients, spec)
    both = jnp.asarray(dft_halves(fft_len))
    cosine, sine = both[:, :fft_len], both[:, fft_len:]
    matrix = jnp.concatenate(
        [jnp.concatenate([cosine, -sine], axis=1), jnp.concatenate([sine, cosine], axis=1)], axis=0
    )
    flat = jnp.transpose(filtered, (1, 2, 0, 3)).reshape(rows * spec, 2 * fft_len)
    product = jnp.dot(flat, matrix, preferred_element_type=jnp.float32).astype(jnp.bfloat16)
    product = product.reshape(rows, spec, 2, fft_len)
    major = jnp.transpose(product, (3, 0, 2, 1)).reshape(fft_len, rows * 2 * spec)
    major = lax.all_to_all(major, "blk", split_axis=0, concat_axis=1, tiled=True)
    major = lax.all_to_all(major, "tch", split_axis=0, concat_axis=1, tiled=True)
    chans = major.shape[0]
    layout = major.reshape(chans, halves, blocks, rows, 2, spec)
    stacked = jnp.transpose(layout, (0, 2, 3, 4, 1, 5)).reshape(chans, inputs, 2 * total)
    target = jnp.arange(inputs, dtype=jnp.int32)
    station_in = jnp.repeat(station_of_slot, POLS) * POLS + target % POLS
    choose = (target[:, None] == station_in[None, :]) & (jnp.repeat(station_ok, POLS) == 1)[:, None]
    ordered = jnp.einsum(
        "ab,cbk->cak", choose.astype(jnp.bfloat16), stacked, preferred_element_type=jnp.float32
    ).astype(jnp.bfloat16)
    turn = jnp.concatenate([-ordered[:, :, total:], ordered[:, :, :total]], axis=2)
    real = jnp.einsum("cak,cbk->cab", ordered, ordered, preferred_element_type=jnp.float32)
    imag = jnp.einsum("cak,cbk->cab", ordered, turn, preferred_element_type=jnp.float32)
    return (jnp.stack([real, imag], axis=0) * (1.0 / total)).astype(jnp.bfloat16)


def local(samples, history, coefficients, station_of_slot, station_ok):
    tap_count, fft_len = coefficients.shape
    rows = samples.shape[1]
    spec = samples.shape[2] // fft_len
    halves = lax.axis_size("tch")
    blocks = lax.axis_size("blk")
    group = blocks * halves
    chans = fft_len // group
    fits = (
        halves == 2
        and group % 4 == 0
        and chans % (16 * ROUNDS) == 0
        and rows % POLS == 0
        and 2 * blocks * rows <= LANES
        and 2 * rows == 8
        and POLS * 2 * spec == LANES
        and tap_count <= spec
        and tap_count % 8 == 0
    )
    form = in_one_kernel if fits else in_parts
    return form(samples, history, coefficients, station_of_slot, station_ok)


def solution(mesh):
    return jax.shard_map(
        local,
        mesh=mesh,
        in_specs=(P("grp", "blk", "tch"), P("grp", "blk", None), P(), P("grp"), P("grp")),
        out_specs=P("grp", ("blk", "tch"), None, None),
        check_vma=False,
    )
```

```python
import functools
import math

import jax
import jax.numpy as jnp
import numpy as np
from jax import lax
from jax.experimental import pallas as pl
from jax.experimental.pallas import tpu as pltpu
from jax.sharding import PartitionSpec as P

POLS = 2
ROUNDS = 2
PAD = 8
LANES = 128
MESH = pl.DeviceIdType.MESH


def by_round(table, group, rounds):
    fft_len = table.shape[0]
    return (
        table.reshape(group, rounds, fft_len // group // rounds, -1)
        .transpose(1, 0, 2, 3)
        .reshape(fft_len, -1)
    )


def dft_halves(fft_len):
    index = np.arange(fft_len)
    phase_step = np.outer(index, index) % fft_len
    angles = phase_step * (2.0 * math.pi / fft_len)
    norm_scale = 1.0 / math.sqrt(fft_len)
    both = np.concatenate([np.cos(angles), np.sin(angles)], axis=1) * norm_scale
    return both.astype(np.float32).astype(jnp.bfloat16)


def kernel(
    blocks,
    halves,
    samples,
    history,
    coefficients,
    table,
    slot_station,
    station_ok,
    out,
    ext,
    wide,
    taps,
    cs,
    filt,
    fed,
    spectra,
    *rest,
):
    landed = rest[:ROUNDS]
    turned, planes, slots, in_sem, own_sem, tail_sem, send_sem, recv_sem = rest[ROUNDS:]
    tap_count, fft_len = coefficients.shape
    rows = samples.shape[1]
    length = samples.shape[2]
    spec = length // fft_len
    past = history.shape[2]
    group = blocks * halves
    chans = fft_len // group
    sub = chans // ROUNDS
    parts = 2 * rows
    pitch = spec + PAD
    stations = slot_station.shape[0]
    inputs = stations * POLS
    deep = 2 * inputs + PAD
    flat = inputs + PAD

    blk = lax.axis_index("blk")
    half = lax.axis_index("tch")
    me = blk * halves + half

    barrier = pltpu.get_barrier_semaphore()

    def greet(step, carry):
        other = lax.rem(me + step, group)
        pl.semaphore_signal(
            barrier,
            inc=1,
            device_id={"blk": other // halves, "tch": other % halves},
            device_id_type=MESH,
        )
        return carry

    lax.fori_loop(1, group, greet, 0)

    get_samples = pltpu.make_async_copy(samples, ext.at[:, :, pl.ds(past, length)], in_sem.at[0])
    get_taps = pltpu.make_async_copy(coefficients, taps, in_sem.at[1])
    get_table = pltpu.make_async_copy(table, cs, in_sem.at[2])
    get_history = pltpu.make_async_copy(history, ext.at[:, :, pl.ds(0, past)], in_sem.at[3])
    get_samples.start()
    get_taps.start()

    @pl.when(half == 0)
    def _():
        get_history.start()

    get_table.start()

    pl.semaphore_wait(barrier, group - 1)

    planes[...] = jnp.zeros_like(planes)

    tail = pltpu.make_async_remote_copy(
        src_ref=samples.at[:, :, pl.ds(length - past, past)],
        dst_ref=ext.at[:, :, pl.ds(0, past)],
        send_sem=tail_sem.at[0],
        recv_sem=tail_sem.at[1],
        device_id={"tch": 1 - half},
        device_id_type=MESH,
    )

    @pl.when(half == 0)
    def _():
        tail.start()

    def widen(first, count):
        def one(m, carry):
            at = pl.ds(pl.multiple_of((first + m) * fft_len, fft_len), fft_len)
            wide[first + m, 0:rows, :] = ext[0, :, at].astype(jnp.float32)
            wide[first + m, rows:parts, :] = ext[1, :, at].astype(jnp.float32)
            return carry

        lax.fori_loop(0, count, one, 0)

    def filter_from(first, count):
        def lane_tile(tile, carry):
            at = pl.ds(pl.multiple_of(tile * LANES, LANES), LANES)
            weight = [
                jnp.broadcast_to(taps[j : j + 1, at], (parts, LANES)) for j in range(tap_count)
            ]
            for base in range(first, first + count, 8):
                sums = [None] * 8
                for m in range(8 + tap_count - 1):
                    block = wide[base + m, :, at]
                    for q in range(8):
                        j = m - q
                        if 0 <= j < tap_count:
                            term = weight[j] * block
                            sums[q] = term if j == 0 else sums[q] + term
                for q in range(8):
                    filt[pl.ds(tile * parts * pitch + base + q, parts, stride=pitch), :] = sums[q]
            return carry

        lax.fori_loop(0, fft_len // LANES, lane_tile, 0)

    early = tap_count
    get_samples.wait()
    get_taps.wait()
    widen(tap_count - 1, spec)
    filter_from(early, spec - early)

    @pl.when(half == 0)
    def _():
        get_history.wait()

    @pl.when(half == 1)
    def _():
        tail.wait_recv()

    widen(0, tap_count - 1)
    filter_from(0, early)

    def feed(tile, carry):
        left = pl.ds(pl.multiple_of(tile * LANES, LANES), LANES)
        right = pl.ds(pl.multiple_of(fft_len + tile * LANES, LANES), LANES)
        base = tile * parts * pitch
        for a in range(rows):
            real_at = pl.ds(pl.multiple_of(base + a * pitch, 8), spec)
            imag_at = pl.ds(pl.multiple_of(base + (rows + a) * pitch, 8), spec)
            real = filt[real_at, :].astype(jnp.bfloat16)
            imag = filt[imag_at, :].astype(jnp.bfloat16)
            top = a * 2 * spec
            fed[top : top + spec, left] = real
            fed[top + spec : top + 2 * spec, left] = imag
            fed[top : top + spec, right] = imag
            fed[top + spec : top + 2 * spec, right] = -real
        return carry

    lax.fori_loop(0, fft_len // LANES, feed, 0)

    def push(turn, device):
        return pltpu.make_async_remote_copy(
            src_ref=spectra.at[turn, device],
            dst_ref=landed[turn].at[me],
            send_sem=send_sem.at[turn],
            recv_sem=recv_sem.at[turn],
            device_id={"blk": device // halves, "tch": device % halves},
            device_id_type=MESH,
        )

    def keep_own(turn):
        return pltpu.make_async_copy(
            spectra.at[turn, me], landed[turn].at[me], own_sem.at[turn]
        )

    per = group // 4
    mine = me // per
    across = lax.rem(mine + 2, 4)
    beside = across + 1 - 2 * lax.rem(across, 2)
    near = mine + 1 - 2 * lax.rem(mine, 2)
    block = fft_len // ROUNDS
    get_table.wait()

    for turn in range(ROUNDS):
        at = slice(turn * block, (turn + 1) * block)
        result = lax.dot_general(
            cs[at, :], fed[...], (((1,), (1,)), ((), ())), preferred_element_type=jnp.float32
        ).astype(jnp.bfloat16)
        for j in range(rows // POLS):
            tile = result[:, j * LANES : (j + 1) * LANES]
            spectra[turn, :, j] = tile.reshape(group, sub, LANES)
        for chunk in (across, beside, near):
            for i in range(per):
                push(turn, chunk * per + lax.rem(me + i, per)).start()
        for i in range(1, per):
            push(turn, mine * per + lax.rem(me + i, per)).start()
        keep_own(turn).start()

    for s in range(stations):
        slot = jnp.int32(0)
        for q in range(stations):
            slot = jnp.where(slot_station[q] == s, q, slot)
        slots[s] = slot

    def whole(turn):
        other = lax.rem(me + 1, group)
        return pltpu.make_async_remote_copy(
            src_ref=spectra.at[turn, pl.ds(0, group - 1)],
            dst_ref=landed[turn].at[pl.ds(0, group - 1)],
            send_sem=send_sem.at[turn],
            recv_sem=recv_sem.at[turn],
            device_id={"blk": other // halves, "tch": other % halves},
            device_id_type=MESH,
        )

    lane = lax.broadcasted_iota(jnp.int32, (sub, LANES), 1)
    low = lane < LANES // 2
    real_lane = lax.rem(lane, LANES // 2) < LANES // 4

    def order(turn, s):
        slot = slots[s]
        source = lax.div(slot, rows // POLS)
        within = lax.rem(slot, rows // POLS)
        keep = station_ok[s].astype(jnp.float32)
        first = landed[turn][source * halves, within].astype(jnp.float32) * keep
        second = landed[turn][source * halves + 1, within].astype(jnp.float32) * keep
        one = jnp.where(low, first, pltpu.roll(second, LANES // 2, 1))
        two = jnp.where(low, pltpu.roll(first, LANES // 2, 1), second)
        for p, value in enumerate((one, two)):
            turned_value = jnp.where(
                real_lane,
                -pltpu.roll(value, LANES - LANES // 4, 1),
                pltpu.roll(value, LANES // 4, 1),
            )
            turned[pl.ds(s * POLS + p, sub, stride=deep), :] = value
            turned[pl.ds(inputs + s * POLS + p, sub, stride=deep), :] = turned_value

    scale = 1.0 / (spec * halves)

    def correlate(turn, c):
        both = turned[c * deep : c * deep + 2 * inputs, :].astype(jnp.bfloat16)
        first = (turn * sub + c) * flat
        planes[pl.ds(pl.multiple_of(first, 8), inputs), 0 : 2 * inputs] = lax.dot_general(
            both[0:inputs, :], both, (((1,), (1,)), ((), ())), preferred_element_type=jnp.float32
        )

    def finish(turn):
        whole(turn).wait_recv()
        keep_own(turn).wait()
        for s in range(stations):
            order(turn, s)
        for c in range(sub):
            correlate(turn, c)

    for turn in range(ROUNDS):
        finish(turn)

    def lay_out(step, carry):
        for i in range(4):
            a = step * 4 + i
            vis = jnp.transpose(planes[pl.ds(a, chans, stride=flat), :] * scale)
            out[0, a] = vis[0:inputs, :].astype(jnp.bfloat16)
            out[1, a] = vis[inputs : 2 * inputs, :].astype(jnp.bfloat16)
        return carry

    lax.fori_loop(0, inputs // 4, lay_out, 0)

    @pl.when(half == 0)
    def _():
        tail.wait_send()

    for turn in range(ROUNDS):
        whole(turn).wait_send()


def in_one_kernel(samples, history, coefficients, station_of_slot, station_ok):
    tap_count, fft_len = coefficients.shape
    rows = samples.shape[1]
    spec = samples.shape[2] // fft_len
    halves = lax.axis_size("tch")
    blocks = lax.axis_size("blk")
    group = blocks * halves
    chans = fft_len // group
    inputs = blocks * rows
    parts = 2 * rows
    table = jnp.asarray(by_round(dft_halves(fft_len), group, ROUNDS))
    sub = chans // ROUNDS
    anywhere = pl.BlockSpec(memory_space=pl.ANY)
    scalars = pl.BlockSpec(memory_space=pltpu.SMEM)
    visibilities = pl.pallas_call(
        functools.partial(kernel, blocks, halves),
        out_shape=jax.ShapeDtypeStruct((2, inputs, inputs, chans), jnp.bfloat16),
        in_specs=[anywhere] * 4 + [scalars] * 2,
        out_specs=pl.BlockSpec(memory_space=pltpu.VMEM),
        scratch_shapes=[
            pltpu.VMEM((2, rows, history.shape[2] + samples.shape[2]), jnp.bfloat16),
            pltpu.VMEM((tap_count - 1 + spec, parts, fft_len), jnp.float32),
            pltpu.VMEM((tap_count, fft_len), jnp.float32),
            pltpu.VMEM((fft_len, 2 * fft_len), jnp.bfloat16),
            pltpu.VMEM((fft_len // LANES * parts * (spec + PAD), LANES), jnp.float32),
            pltpu.VMEM((parts * spec, 2 * fft_len), jnp.bfloat16),
            pltpu.VMEM((ROUNDS, group, rows // POLS, sub, LANES), jnp.bfloat16),
            *[pltpu.VMEM((group, rows // POLS, sub, LANES), jnp.bfloat16)] * ROUNDS,
            pltpu.VMEM((sub * (2 * inputs + PAD), LANES), jnp.float32),
            pltpu.VMEM((chans * (inputs + PAD), LANES), jnp.float32),
            pltpu.SMEM((inputs // POLS,), jnp.int32),
            pltpu.SemaphoreType.DMA((4,)),
            pltpu.SemaphoreType.DMA((ROUNDS,)),
            pltpu.SemaphoreType.DMA((2,)),
            pltpu.SemaphoreType.DMA((ROUNDS,)),
            pltpu.SemaphoreType.DMA((ROUNDS,)),
        ],
        compiler_params=pltpu.CompilerParams(
            collective_id=0, has_side_effects=True, vmem_limit_bytes=62 * 2**20
        ),
    )(samples, history, coefficients, table, station_of_slot, station_ok)
    return jnp.transpose(visibilities, (0, 3, 1, 2))


def filter_bank(extended, coefficients, spec_count):
    tap_count, fft_len = coefficients.shape
    blocks = extended.reshape(extended.shape[0], extended.shape[1], -1, fft_len)
    running = jnp.zeros((extended.shape[0], extended.shape[1], spec_count, fft_len), jnp.float32)
    for j in range(tap_count):
        running = running + coefficients[j] * blocks[:, :, j : j + spec_count, :].astype(jnp.float32)
    return running.astype(jnp.bfloat16)


def in_parts(samples, history, coefficients, station_of_slot, station_ok):
    tap_count, fft_len = coefficients.shape
    rows = samples.shape[1]
    spec = samples.shape[2] // fft_len
    halves = lax.axis_size("tch")
    blocks = lax.axis_size("blk")
    inputs = blocks * rows
    total = spec * halves
    past = (tap_count - 1) * fft_len
    ends = jnp.concatenate([history, samples], axis=2)[:, :, -past:]
    earlier = lax.ppermute(ends, "tch", [(i, i + 1) for i in range(halves - 1)])
    earlier = jnp.where(lax.axis_index("tch") == 0, history, earlier)
    filtered = filter_bank(jnp.concatenate([earlier, samples], axis=2), coefficients, spec)
    both = jnp.asarray(dft_halves(fft_len))
    cosine, sine = both[:, :fft_len], both[:, fft_len:]
    matrix = jnp.concatenate(
        [jnp.concatenate([cosine, -sine], axis=1), jnp.concatenate([sine, cosine], axis=1)], axis=0
    )
    flat = jnp.transpose(filtered, (1, 2, 0, 3)).reshape(rows * spec, 2 * fft_len)
    product = jnp.dot(flat, matrix, preferred_element_type=jnp.float32).astype(jnp.bfloat16)
    product = product.reshape(rows, spec, 2, fft_len)
    major = jnp.transpose(product, (3, 0, 2, 1)).reshape(fft_len, rows * 2 * spec)
    major = lax.all_to_all(major, "blk", split_axis=0, concat_axis=1, tiled=True)
    major = lax.all_to_all(major, "tch", split_axis=0, concat_axis=1, tiled=True)
    chans = major.shape[0]
    layout = major.reshape(chans, halves, blocks, rows, 2, spec)
    stacked = jnp.transpose(layout, (0, 2, 3, 4, 1, 5)).reshape(chans, inputs, 2 * total)
    target = jnp.arange(inputs, dtype=jnp.int32)
    station_in = jnp.repeat(station_of_slot, POLS) * POLS + target % POLS
    choose = (target[:, None] == station_in[None, :]) & (jnp.repeat(station_ok, POLS) == 1)[:, None]
    ordered = jnp.einsum(
        "ab,cbk->cak", choose.astype(jnp.bfloat16), stacked, preferred_element_type=jnp.float32
    ).astype(jnp.bfloat16)
    turn = jnp.concatenate([-ordered[:, :, total:], ordered[:, :, :total]], axis=2)
    real = jnp.einsum("cak,cbk->cab", ordered, ordered, preferred_element_type=jnp.float32)
    imag = jnp.einsum("cak,cbk->cab", ordered, turn, preferred_element_type=jnp.float32)
    return (jnp.stack([real, imag], axis=0) * (1.0 / total)).astype(jnp.bfloat16)


def local(samples, history, coefficients, station_of_slot, station_ok):
    tap_count, fft_len = coefficients.shape
    rows = samples.shape[1]
    spec = samples.shape[2] // fft_len
    halves = lax.axis_size("tch")
    blocks = lax.axis_size("blk")
    group = blocks * halves
    chans = fft_len // group
    fits = (
        halves == 2
        and group % 4 == 0
        and chans % (16 * ROUNDS) == 0
        and rows % POLS == 0
        and 2 * blocks * rows <= LANES
        and 2 * rows == 8
        and POLS * 2 * spec == LANES
        and tap_count <= spec
        and tap_count % 8 == 0
    )
    form = in_one_kernel if fits else in_parts
    return form(samples, history, coefficients, station_of_slot, station_ok)


def solution(mesh):
    return jax.shard_map(
        local,
        mesh=mesh,
        in_specs=(P("grp", "blk", "tch"), P("grp", "blk", None), P(), P("grp"), P("grp")),
        out_specs=P("grp", ("blk", "tch"), None, None),
        check_vma=False,
    )
```

```python
import functools
import math

import jax
import jax.numpy as jnp
import numpy as np
from jax import lax
from jax.experimental import pallas as pl
from jax.experimental.pallas import tpu as pltpu
from jax.sharding import PartitionSpec as P

POLS = 2
ROUNDS = 2
PAD = 8
LANES = 128
MESH = pl.DeviceIdType.MESH


def by_round(table, group, rounds):
    fft_len = table.shape[0]
    return (
        table.reshape(group, rounds, fft_len // group // rounds, -1)
        .transpose(1, 0, 2, 3)
        .reshape(fft_len, -1)
    )


def dft_halves(fft_len):
    index = np.arange(fft_len)
    phase_step = np.outer(index, index) % fft_len
    angles = phase_step * (2.0 * math.pi / fft_len)
    norm_scale = 1.0 / math.sqrt(fft_len)
    both = np.concatenate([np.cos(angles), np.sin(angles)], axis=1) * norm_scale
    return both.astype(np.float32).astype(jnp.bfloat16)


def kernel(
    blocks,
    halves,
    samples,
    history,
    coefficients,
    table,
    slot_station,
    station_ok,
    planes,
    ext,
    wide,
    taps,
    cs,
    filt,
    fed,
    spectra,
    *rest,
):
    landed = rest[:ROUNDS]
    turned, slots, in_sem, own_sem, tail_sem, send_sem, recv_sem = rest[ROUNDS:]
    tap_count, fft_len = coefficients.shape
    rows = samples.shape[1]
    length = samples.shape[2]
    spec = length // fft_len
    past = history.shape[2]
    group = blocks * halves
    chans = fft_len // group
    sub = chans // ROUNDS
    parts = 2 * rows
    pitch = spec + PAD
    stations = slot_station.shape[0]
    inputs = stations * POLS
    deep = 2 * inputs + PAD
    flat = inputs + PAD

    blk = lax.axis_index("blk")
    half = lax.axis_index("tch")
    me = blk * halves + half

    barrier = pltpu.get_barrier_semaphore()

    def greet(step, carry):
        other = lax.rem(me + step, group)
        pl.semaphore_signal(
            barrier,
            inc=1,
            device_id={"blk": other // halves, "tch": other % halves},
            device_id_type=MESH,
        )
        return carry

    lax.fori_loop(1, group, greet, 0)

    get_samples = pltpu.make_async_copy(samples, ext.at[:, :, pl.ds(past, length)], in_sem.at[0])
    get_taps = pltpu.make_async_copy(coefficients, taps, in_sem.at[1])
    get_table = pltpu.make_async_copy(table, cs, in_sem.at[2])
    get_history = pltpu.make_async_copy(history, ext.at[:, :, pl.ds(0, past)], in_sem.at[3])
    get_samples.start()
    get_taps.start()

    @pl.when(half == 0)
    def _():
        get_history.start()

    get_table.start()

    def widen(first, count):
        def one(m, carry):
            at = pl.ds(pl.multiple_of((first + m) * fft_len, fft_len), fft_len)
            wide[first + m, 0:rows, :] = ext[0, :, at].astype(jnp.float32)
            wide[first + m, rows:parts, :] = ext[1, :, at].astype(jnp.float32)
            return carry

        lax.fori_loop(0, count, one, 0)

    planes[...] = jnp.zeros_like(planes)
    get_samples.wait()
    widen(tap_count - 1, spec)
    pl.semaphore_wait(barrier, group - 1)

    tail = pltpu.make_async_remote_copy(
        src_ref=samples.at[:, :, pl.ds(length - past, past)],
        dst_ref=ext.at[:, :, pl.ds(0, past)],
        send_sem=tail_sem.at[0],
        recv_sem=tail_sem.at[1],
        device_id={"tch": 1 - half},
        device_id_type=MESH,
    )

    @pl.when(half == 0)
    def _():
        tail.start()

    def filter_from(first, count):
        def lane_tile(tile, carry):
            at = pl.ds(pl.multiple_of(tile * LANES, LANES), LANES)
            weight = [
                jnp.broadcast_to(taps[j : j + 1, at], (parts, LANES)) for j in range(tap_count)
            ]
            for base in range(first, first + count, 8):
                sums = [None] * 8
                for m in range(8 + tap_count - 1):
                    block = wide[base + m, :, at]
                    for q in range(8):
                        j = m - q
                        if 0 <= j < tap_count:
                            term = weight[j] * block
                            sums[q] = term if j == 0 else sums[q] + term
                for q in range(8):
                    filt[pl.ds(tile * parts * pitch + base + q, parts, stride=pitch), :] = sums[q]
            return carry

        lax.fori_loop(0, fft_len // LANES, lane_tile, 0)

    early = tap_count
    get_taps.wait()
    filter_from(early, spec - early)

    @pl.when(half == 0)
    def _():
        get_history.wait()

    @pl.when(half == 1)
    def _():
        tail.wait_recv()

    widen(0, tap_count - 1)
    filter_from(0, early)

    def feed(tile, carry):
        left = pl.ds(pl.multiple_of(tile * LANES, LANES), LANES)
        right = pl.ds(pl.multiple_of(fft_len + tile * LANES, LANES), LANES)
        base = tile * parts * pitch
        for a in range(rows):
            real_at = pl.ds(pl.multiple_of(base + a * pitch, 8), spec)
            imag_at = pl.ds(pl.multiple_of(base + (rows + a) * pitch, 8), spec)
            real = filt[real_at, :].astype(jnp.bfloat16)
            imag = filt[imag_at, :].astype(jnp.bfloat16)
            top = a * 2 * spec
            fed[top : top + spec, left] = real
            fed[top + spec : top + 2 * spec, left] = imag
            fed[top : top + spec, right] = imag
            fed[top + spec : top + 2 * spec, right] = -real
        return carry

    lax.fori_loop(0, fft_len // LANES, feed, 0)

    def push(turn, device):
        return pltpu.make_async_remote_copy(
            src_ref=spectra.at[turn, device],
            dst_ref=landed[turn].at[me],
            send_sem=send_sem.at[turn],
            recv_sem=recv_sem.at[turn],
            device_id={"blk": device // halves, "tch": device % halves},
            device_id_type=MESH,
        )

    def keep_own(turn):
        return pltpu.make_async_copy(
            spectra.at[turn, me], landed[turn].at[me], own_sem.at[turn]
        )

    per = group // 4
    mine = me // per
    across = lax.rem(mine + 2, 4)
    beside = across + 1 - 2 * lax.rem(across, 2)
    near = mine + 1 - 2 * lax.rem(mine, 2)
    block = fft_len // ROUNDS
    get_table.wait()

    for turn in range(ROUNDS):
        at = slice(turn * block, (turn + 1) * block)
        result = lax.dot_general(
            cs[at, :], fed[...], (((1,), (1,)), ((), ())), preferred_element_type=jnp.float32
        ).astype(jnp.bfloat16)
        for j in range(rows // POLS):
            tile = result[:, j * LANES : (j + 1) * LANES]
            spectra[turn, :, j] = tile.reshape(group, sub, LANES)
        for chunk in (across, beside, near):
            for i in range(per):
                push(turn, chunk * per + lax.rem(me + i, per)).start()
        for i in range(1, per):
            push(turn, mine * per + lax.rem(me + i, per)).start()
        keep_own(turn).start()

    for s in range(stations):
        slot = jnp.int32(0)
        for q in range(stations):
            slot = jnp.where(slot_station[q] == s, q, slot)
        slots[s] = slot

    def whole(turn):
        other = lax.rem(me + 1, group)
        return pltpu.make_async_remote_copy(
            src_ref=spectra.at[turn, pl.ds(0, group - 1)],
            dst_ref=landed[turn].at[pl.ds(0, group - 1)],
            send_sem=send_sem.at[turn],
            recv_sem=recv_sem.at[turn],
            device_id={"blk": other // halves, "tch": other % halves},
            device_id_type=MESH,
        )

    lane = lax.broadcasted_iota(jnp.int32, (sub, LANES), 1)
    low = lane < LANES // 2
    real_lane = lax.rem(lane, LANES // 2) < LANES // 4

    def order(turn, s):
        slot = slots[s]
        source = lax.div(slot, rows // POLS)
        within = lax.rem(slot, rows // POLS)
        keep = station_ok[s].astype(jnp.float32)
        first = landed[turn][source * halves, within].astype(jnp.float32) * keep
        second = landed[turn][source * halves + 1, within].astype(jnp.float32) * keep
        one = jnp.where(low, first, pltpu.roll(second, LANES // 2, 1))
        two = jnp.where(low, pltpu.roll(first, LANES // 2, 1), second)
        for p, value in enumerate((one, two)):
            turned_value = jnp.where(
                real_lane,
                -pltpu.roll(value, LANES - LANES // 4, 1),
                pltpu.roll(value, LANES // 4, 1),
            )
            turned[pl.ds(s * POLS + p, sub, stride=deep), :] = value
            turned[pl.ds(inputs + s * POLS + p, sub, stride=deep), :] = turned_value

    def correlate(turn, c):
        both = turned[c * deep : c * deep + 2 * inputs, :].astype(jnp.bfloat16)
        first = (turn * sub + c) * flat
        planes[pl.ds(pl.multiple_of(first, 8), inputs), 0 : 2 * inputs] = lax.dot_general(
            both[0:inputs, :], both, (((1,), (1,)), ((), ())), preferred_element_type=jnp.float32
        )

    def finish(turn):
        whole(turn).wait_recv()
        keep_own(turn).wait()
        for s in range(stations):
            order(turn, s)
        for c in range(sub):
            correlate(turn, c)

    for turn in range(ROUNDS):
        finish(turn)

    @pl.when(half == 0)
    def _():
        tail.wait_send()

    for turn in range(ROUNDS):
        whole(turn).wait_send()


def channels_minor(scale, planes, out):
    inputs = out.shape[1]
    chans = out.shape[3]
    flat = planes.shape[0] // chans
    for a in range(inputs):
        vis = jnp.transpose(planes[pl.ds(a, chans, stride=flat), :] * scale)
        out[0, a] = vis[0:inputs, :].astype(jnp.bfloat16)
        out[1, a] = vis[inputs : 2 * inputs, :].astype(jnp.bfloat16)


def in_one_kernel(samples, history, coefficients, station_of_slot, station_ok):
    tap_count, fft_len = coefficients.shape
    rows = samples.shape[1]
    spec = samples.shape[2] // fft_len
    halves = lax.axis_size("tch")
    blocks = lax.axis_size("blk")
    group = blocks * halves
    chans = fft_len // group
    inputs = blocks * rows
    parts = 2 * rows
    table = jnp.asarray(by_round(dft_halves(fft_len), group, ROUNDS))
    sub = chans // ROUNDS
    anywhere = pl.BlockSpec(memory_space=pl.ANY)
    scalars = pl.BlockSpec(memory_space=pltpu.SMEM)
    planes = pl.pallas_call(
        functools.partial(kernel, blocks, halves),
        out_shape=jax.ShapeDtypeStruct((chans * (inputs + PAD), LANES), jnp.float32),
        in_specs=[anywhere] * 4 + [scalars] * 2,
        out_specs=pl.BlockSpec(memory_space=pltpu.VMEM),
        scratch_shapes=[
            pltpu.VMEM((2, rows, history.shape[2] + samples.shape[2]), jnp.bfloat16),
            pltpu.VMEM((tap_count - 1 + spec, parts, fft_len), jnp.float32),
            pltpu.VMEM((tap_count, fft_len), jnp.float32),
            pltpu.VMEM((fft_len, 2 * fft_len), jnp.bfloat16),
            pltpu.VMEM((fft_len // LANES * parts * (spec + PAD), LANES), jnp.float32),
            pltpu.VMEM((parts * spec, 2 * fft_len), jnp.bfloat16),
            pltpu.VMEM((ROUNDS, group, rows // POLS, sub, LANES), jnp.bfloat16),
            *[pltpu.VMEM((group, rows // POLS, sub, LANES), jnp.bfloat16)] * ROUNDS,
            pltpu.VMEM((sub * (2 * inputs + PAD), LANES), jnp.float32),
            pltpu.SMEM((inputs // POLS,), jnp.int32),
            pltpu.SemaphoreType.DMA((4,)),
            pltpu.SemaphoreType.DMA((ROUNDS,)),
            pltpu.SemaphoreType.DMA((2,)),
            pltpu.SemaphoreType.DMA((ROUNDS,)),
            pltpu.SemaphoreType.DMA((ROUNDS,)),
        ],
        compiler_params=pltpu.CompilerParams(
            collective_id=0, has_side_effects=True, vmem_limit_bytes=62 * 2**20
        ),
    )(samples, history, coefficients, table, station_of_slot, station_ok)
    visibilities = pl.pallas_call(
        functools.partial(channels_minor, 1.0 / (spec * halves)),
        out_shape=jax.ShapeDtypeStruct((2, inputs, inputs, chans), jnp.bfloat16),
        in_specs=[pl.BlockSpec(memory_space=pltpu.VMEM)],
        out_specs=pl.BlockSpec(memory_space=pltpu.VMEM),
    )(planes)
    return jnp.transpose(visibilities, (0, 3, 1, 2))


def filter_bank(extended, coefficients, spec_count):
    tap_count, fft_len = coefficients.shape
    blocks = extended.reshape(extended.shape[0], extended.shape[1], -1, fft_len)
    running = jnp.zeros((extended.shape[0], extended.shape[1], spec_count, fft_len), jnp.float32)
    for j in range(tap_count):
        running = running + coefficients[j] * blocks[:, :, j : j + spec_count, :].astype(jnp.float32)
    return running.astype(jnp.bfloat16)


def in_parts(samples, history, coefficients, station_of_slot, station_ok):
    tap_count, fft_len = coefficients.shape
    rows = samples.shape[1]
    spec = samples.shape[2] // fft_len
    halves = lax.axis_size("tch")
    blocks = lax.axis_size("blk")
    inputs = blocks * rows
    total = spec * halves
    past = (tap_count - 1) * fft_len
    ends = jnp.concatenate([history, samples], axis=2)[:, :, -past:]
    earlier = lax.ppermute(ends, "tch", [(i, i + 1) for i in range(halves - 1)])
    earlier = jnp.where(lax.axis_index("tch") == 0, history, earlier)
    filtered = filter_bank(jnp.concatenate([earlier, samples], axis=2), coefficients, spec)
    both = jnp.asarray(dft_halves(fft_len))
    cosine, sine = both[:, :fft_len], both[:, fft_len:]
    matrix = jnp.concatenate(
        [jnp.concatenate([cosine, -sine], axis=1), jnp.concatenate([sine, cosine], axis=1)], axis=0
    )
    flat = jnp.transpose(filtered, (1, 2, 0, 3)).reshape(rows * spec, 2 * fft_len)
    product = jnp.dot(flat, matrix, preferred_element_type=jnp.float32).astype(jnp.bfloat16)
    product = product.reshape(rows, spec, 2, fft_len)
    major = jnp.transpose(product, (3, 0, 2, 1)).reshape(fft_len, rows * 2 * spec)
    major = lax.all_to_all(major, "blk", split_axis=0, concat_axis=1, tiled=True)
    major = lax.all_to_all(major, "tch", split_axis=0, concat_axis=1, tiled=True)
    chans = major.shape[0]
    layout = major.reshape(chans, halves, blocks, rows, 2, spec)
    stacked = jnp.transpose(layout, (0, 2, 3, 4, 1, 5)).reshape(chans, inputs, 2 * total)
    target = jnp.arange(inputs, dtype=jnp.int32)
    station_in = jnp.repeat(station_of_slot, POLS) * POLS + target % POLS
    choose = (target[:, None] == station_in[None, :]) & (jnp.repeat(station_ok, POLS) == 1)[:, None]
    ordered = jnp.einsum(
        "ab,cbk->cak", choose.astype(jnp.bfloat16), stacked, preferred_element_type=jnp.float32
    ).astype(jnp.bfloat16)
    turn = jnp.concatenate([-ordered[:, :, total:], ordered[:, :, :total]], axis=2)
    real = jnp.einsum("cak,cbk->cab", ordered, ordered, preferred_element_type=jnp.float32)
    imag = jnp.einsum("cak,cbk->cab", ordered, turn, preferred_element_type=jnp.float32)
    return (jnp.stack([real, imag], axis=0) * (1.0 / total)).astype(jnp.bfloat16)


def local(samples, history, coefficients, station_of_slot, station_ok):
    tap_count, fft_len = coefficients.shape
    rows = samples.shape[1]
    spec = samples.shape[2] // fft_len
    halves = lax.axis_size("tch")
    blocks = lax.axis_size("blk")
    group = blocks * halves
    chans = fft_len // group
    fits = (
        halves == 2
        and group % 4 == 0
        and chans % (16 * ROUNDS) == 0
        and rows % POLS == 0
        and 2 * blocks * rows <= LANES
        and 2 * rows == 8
        and POLS * 2 * spec == LANES
        and tap_count <= spec
        and tap_count % 8 == 0
    )
    form = in_one_kernel if fits else in_parts
    return form(samples, history, coefficients, station_of_slot, station_ok)


def solution(mesh):
    return jax.shard_map(
        local,
        mesh=mesh,
        in_specs=(P("grp", "blk", "tch"), P("grp", "blk", None), P(), P("grp"), P("grp")),
        out_specs=P("grp", ("blk", "tch"), None, None),
        check_vma=False,
    )
```
